256 devices in a mesh: tm: 8 (over z), chan: 32 (over x, y, core).
Axes of the slice: x: 4, y: 4, z: 8, core: 2. Of those that a mesh axis runs over, the one named last changes fastest.
Arguments:
- traces: bfloat16 [8192, 32768], P('chan', 'tm'), may hold values from -80 to 80
- band_edges: int32 [32, 2], P('tm'), may hold values from 0 to 256, as said below
- slot_pairs: int32 [320, 2], P('chan'), may hold values from -1 to 63, as said below
Outputs:
- cross_spectra: float32 [320, 32, 2, 128, 128], P('chan', 'tm')
The draws below stay inside these ranges and needn't reach their ends.
Inputs may be any that keep to these rules, and one draw needn't show every extreme that they name: `band_edges`: row k holds the first bin and one past the last bin of band k; the bands tile the bins 0 to 255 in order, each one bin wide or more, and the bands k * 4 to (k + 1) * 4 - 1 cover exactly the bins k * 32 to (k + 1) * 32 - 1. `slot_pairs`: row r = o * 5 + s belongs to block o; it holds a pair (a, b) with a <= b <= a + 2 and o equal to a or to b, or (-1, -1) for an empty row. No pair appears twice. In every draw some block fills all 5 of its rows; the other blocks own uneven numbers of pairs, in rows of any order.
All inputs are finite; a program needn't handle non-finite values.
Results may differ from the reference program's by a relative error of at most 0.0037.
Values may be sent and summed in bfloat16 or wider, within the bound.
A program may use at most 128 MiB of HBM per device.

```python
import math
import jax
import jax.numpy as jnp
import numpy as np
from jax import lax

CB = 128
SEG = 512
NF = 256
BANDS = 32
SMOOTH = 64
REACH = 2
NBLK = 64
NCH = 8192
NT = 32768
NSEG = 128
NFS = 32
BANDS_DEV = 4
CAP = 5


def draw_traces(key, part):
    key = jax.random.fold_in(key, 11)
    noise_key, gain_key, tone_key, phase_key, amp_key = jax.random.split(key, 5)
    gains = jnp.exp(jax.random.uniform(gain_key, (NCH, 1), jnp.float32, 0.0, math.log(10.0)))
    tone_bins = jax.random.randint(tone_key, (NCH, 1), 4, NF - 4)
    sample_ids = jnp.arange(NT, dtype=jnp.int32)[None, :]
    phases = (tone_bins * sample_ids % SEG).astype(jnp.float32) * (2.0 * math.pi / SEG)
    offsets = jax.random.uniform(phase_key, (NCH, 1), jnp.float32, -math.pi, math.pi)
    amplitudes = jax.random.uniform(amp_key, (NCH, 1), jnp.float32, 0.0, 3.0)
    tone_part = amplitudes * jnp.cos(phases + offsets)
    noise_part = jnp.clip(jax.random.normal(noise_key, (NCH, NT), jnp.float32), -4.0, 4.0)
    return (gains * (noise_part + tone_part)).astype(jnp.bfloat16)


def draw_band_edges(key, part):
    key = jax.random.fold_in(key, 23)
    run_count = BANDS // BANDS_DEV
    run_keys = jax.random.split(key, run_count)

    def one_run(run_key):
        shuffled = jax.random.permutation(run_key, NFS - 1)
        cuts = jnp.sort(shuffled[:BANDS_DEV - 1]).astype(jnp.int32) + 1
        return jnp.concatenate([jnp.zeros((1,), jnp.int32), cuts, jnp.full((1,), NFS, jnp.int32)])
    edges = jax.vmap(one_run)(run_keys) + (jnp.arange(run_count, dtype=jnp.int32) * NFS)[:, None]
    return jnp.stack([edges[:, :-1].reshape(-1), edges[:, 1:].reshape(-1)], axis=1)


def draw_slot_pairs(key, part):
    key = jax.random.fold_in(key, 37)
    include_key, owner_key, forced_key, order_key = jax.random.split(key, 4)
    step_ids = jnp.arange(REACH + 1, dtype=jnp.int32)[None, :]
    block_ids = jnp.arange(NBLK, dtype=jnp.int32)[:, None]
    included = jax.random.randint(include_key, (NBLK, REACH + 1), 0, 20) < 17
    upper_owns = jax.random.randint(owner_key, (NBLK, REACH + 1), 0, 2) == 1
    forced = jax.random.randint(forced_key, (), REACH, NBLK - REACH)
    touch_lower = block_ids == forced
    touch_upper = (block_ids + step_ids == forced) & (step_ids > 0)
    included = (included | touch_lower | touch_upper) & (block_ids + step_ids < NBLK)
    upper_owns = jnp.where(touch_lower, False, jnp.where(touch_upper, True, upper_owns)) & (step_ids > 0)
    offsets = jnp.arange(2 * REACH + 1, dtype=jnp.int32)[None, :] - REACH
    lower_block = jnp.where(offsets >= 0, block_ids, block_ids + offsets)
    distance = jnp.abs(offsets) + jnp.zeros_like(block_ids)
    upper_block = lower_block + distance
    in_range = (lower_block >= 0) & (upper_block < NBLK)
    safe_lower = jnp.clip(lower_block, 0, NBLK - 1)
    picked = included[safe_lower, distance] & in_range
    owned = jnp.where(offsets >= 0, jnp.logical_not(upper_owns[safe_lower, distance]), upper_owns[safe_lower, distance])
    is_live = picked & owned
    pairs = jnp.stack([jnp.where(is_live, lower_block, -1), jnp.where(is_live, upper_block, -1)], axis=2)

    def row_order(row_key):
        return jax.random.permutation(row_key, CAP)
    orders = jax.vmap(row_order)(jax.random.split(order_key, NBLK))
    placed = jnp.take_along_axis(pairs, orders[:, :, None], axis=1)
    return placed.reshape(NBLK * CAP, 2).astype(jnp.int32)


def setup_inputs(seed: int = 0) -> dict:
    key_list = jax.random.split(jax.random.key(seed), 4)
    return {
        "traces": draw_traces(jax.random.fold_in(key_list[3], 71), 0),
        "band_edges": draw_band_edges(jax.random.fold_in(key_list[3], 71), 0),
        "slot_pairs": draw_slot_pairs(jax.random.fold_in(key_list[3], 71), 0),
    }


whiten_eps = 1e-06

def transform_tables(seg_len, bin_count):
    sample_ids = jnp.arange(seg_len, dtype=jnp.int32)[:, None]
    bin_ids = jnp.arange(bin_count, dtype=jnp.int32)[None, :]
    phases = (sample_ids * bin_ids % seg_len).astype(jnp.float32) * (2.0 * math.pi / seg_len)
    hann_taper = 0.5 - 0.5 * jnp.cos(jnp.arange(seg_len, dtype=jnp.float32) * (2.0 * math.pi / seg_len))
    cosine = hann_taper[:, None] * jnp.cos(phases)
    sine_part = -hann_taper[:, None] * jnp.sin(phases)
    return jnp.stack([cosine, sine_part]).astype(jnp.bfloat16)

def window_mean(power, axis, bin_count, half_width):
    totals = jnp.cumsum(power, axis=axis)
    front_shape = list(power.shape)
    front_shape[axis] = half_width + 1
    front = jnp.zeros(tuple(front_shape), power.dtype)
    last_total = lax.slice_in_dim(totals, bin_count - 1, bin_count, axis=axis)
    back_shape = list(power.shape)
    back_shape[axis] = half_width
    back = jnp.broadcast_to(last_total, tuple(back_shape))
    extended = jnp.concatenate([front, totals, back], axis=axis)
    upper_part = lax.slice_in_dim(extended, 2 * half_width + 1, 2 * half_width + 1 + bin_count, axis=axis)
    lower_part = lax.slice_in_dim(extended, 0, bin_count, axis=axis)
    bin_ids = np.arange(bin_count)
    window_count = (np.minimum(bin_ids + half_width + 1, bin_count) - np.maximum(bin_ids - half_width, 0)).astype(np.float32)
    count_shape = [1] * power.ndim
    count_shape[axis] = bin_count
    counts = jnp.asarray(window_count.reshape(count_shape), power.dtype)
    return (upper_part - lower_part) / counts

def band_weights(band_edges, bin_ids, segment_count):
    lower_edge = band_edges[:, 0:1]
    upper_edge = band_edges[:, 1:2]
    inside = ((bin_ids[None, :] >= lower_edge) & (bin_ids[None, :] < upper_edge)).astype(jnp.float32)
    band_width = (upper_edge - lower_edge).astype(jnp.float32)
    return inside / jnp.sqrt(segment_count * band_width)

def whiten_frames(frames, tables):
    spectra = jnp.einsum('csn,pnf->psfc', frames.astype(jnp.float32), tables.astype(jnp.float32), precision=lax.Precision.HIGHEST)
    spectral_power = spectra[0] * spectra[0] + spectra[1] * spectra[1]
    smooth = window_mean(spectral_power, 1, NF, SMOOTH)
    return (spectra * lax.rsqrt(smooth + whiten_eps)[None]).astype(jnp.bfloat16)

def pair_cross(left_side, right_side, weights):
    left_f32 = left_side.astype(jnp.float32)
    right_f32 = right_side.astype(jnp.float32)
    swapped = jnp.stack([left_f32[1], -left_f32[0]])
    real_part = jnp.einsum('psfi,psfj->fij', left_f32, right_f32, precision=lax.Precision.HIGHEST)
    imag_part = jnp.einsum('psfi,psfj->fij', swapped, right_f32, precision=lax.Precision.HIGHEST)
    stacked = jnp.stack([real_part, imag_part])
    return jnp.einsum('kf,qfij->kqij', weights, stacked, precision=lax.Precision.HIGHEST)

def reference(traces, band_edges, slot_pairs):
    tables = transform_tables(SEG, NF)
    half_seg = SEG // 2

    def block_spectra(block_rows):
        padded = jnp.pad(block_rows, ((0, 0), (0, half_seg)))
        halves = padded.reshape(CB, NSEG + 1, half_seg)
        frames = jnp.concatenate([halves[:, :-1], halves[:, 1:]], axis=2)
        return whiten_frames(frames, tables)
    whitened = lax.map(block_spectra, traces.reshape(NBLK, CB, NT))
    weights = band_weights(band_edges, jnp.arange(NF, dtype=jnp.int32), NSEG)

    def one_slot(slot_pair):
        first_block = jnp.maximum(slot_pair[0], 0).astype(jnp.int32)
        second_block = jnp.maximum(slot_pair[1], 0).astype(jnp.int32)
        left_side = lax.dynamic_index_in_dim(whitened, first_block, 0, keepdims=False)
        right_side = lax.dynamic_index_in_dim(whitened, second_block, 0, keepdims=False)
        result = pair_cross(left_side, right_side, weights)
        return jnp.where(slot_pair[0] >= 0, result, jnp.zeros_like(result))
    return lax.map(one_slot, slot_pairs)
```

```python
import functools

import jax
import jax.numpy as jnp
import numpy as np
from jax import lax
from jax.experimental import pallas as pl
from jax.experimental.pallas import tpu as pltpu
from jax.sharding import PartitionSpec as P

CB = 128
SEG = 512
HALF = 256
NF = 256
SMOOTH = 64
LANES = 128
RUNS = 8
BINS = 32
GROUPS = 4
JG = 4
BANDS_DEV = 4
ROWS = 10
HOPS = (0, 4, 3, 5, 2, 6, 1, 7)

whiten_eps = 1e-06
MESH = pl.DeviceIdType.MESH


def constant_tables():
    n = np.arange(SEG)[:, None].astype(np.int64)
    f = np.arange(NF)[None, :].astype(np.int64)
    phase = (n * f % SEG).astype(np.float64) * (2.0 * np.pi / SEG)
    taper = 0.5 - 0.5 * np.cos(np.arange(SEG).astype(np.float64) * (2.0 * np.pi / SEG))
    tables = np.concatenate([taper[:, None] * np.cos(phase), -taper[:, None] * np.sin(phase)], axis=1)
    bins = np.arange(NF)
    near = (np.abs(bins[:, None] - bins[None, :]) <= SMOOTH).astype(np.float32)
    counts = near.sum(axis=0)
    inverse = np.broadcast_to((1.0 / counts).astype(np.float32)[None, :], (8, NF))
    return (
        jnp.asarray(tables.astype(np.float32), jnp.bfloat16),
        jnp.asarray(near, jnp.bfloat16),
        jnp.asarray(inverse, jnp.float32),
    )


def kernel(
    edges, slots, traces, tables, near, inverse, out,
    xh, tab, ban, inv, spec, send, big, acc, masks, stage,
    load_sem, halo_sem, out_sem, send_sem, recv_sem, fsend_sem, frecv_sem,
):
    t = lax.axis_index("tm")
    ch = lax.axis_index("chan")
    chans = 32
    samples = 4096

    loads = [
        pltpu.make_async_copy(tables, tab, load_sem.at[0]),
        pltpu.make_async_copy(near, ban, load_sem.at[1]),
        pltpu.make_async_copy(inverse, inv, load_sem.at[2]),
        pltpu.make_async_copy(traces, xh.at[:, pl.ds(0, samples)], load_sem.at[3]),
    ]
    for load in loads:
        load.start()

    def tm_at(step):
        return lax.rem(t + step, RUNS)

    right = lax.rem(ch + 1, chans)
    left = lax.rem(ch + chans - 1, chans)

    barrier = pltpu.get_barrier_semaphore()
    for hop in range(1, RUNS):
        pl.semaphore_signal(barrier, inc=1, device_id=(tm_at(hop), ch), device_id_type=MESH)
    pl.semaphore_signal(barrier, inc=1, device_id=(t, right), device_id_type=MESH)
    pl.semaphore_signal(barrier, inc=1, device_id=(t, left), device_id_type=MESH)
    pl.semaphore_wait(barrier, RUNS + 1)

    halo = pltpu.make_async_remote_copy(
        src_ref=traces.at[:, pl.ds(0, HALF)],
        dst_ref=xh.at[:, pl.ds(samples, HALF)],
        send_sem=halo_sem.at[0],
        recv_sem=halo_sem.at[1],
        device_id=(tm_at(RUNS - 1), ch),
        device_id_type=MESH,
    )
    halo.start()
    for load in loads:
        load.wait()

    def run_copy(place, g, b):
        run = tm_at(HOPS[place])
        return pltpu.make_async_remote_copy(
            src_ref=send.at[run, g, b],
            dst_ref=big.at[place, g, 2 + b],
            send_sem=send_sem.at[place, g, b],
            recv_sem=recv_sem.at[place, g, b],
            device_id=(run, ch),
            device_id_type=MESH,
        )

    def own_copy(g, b):
        return pltpu.make_async_copy(send.at[t, g, b], big.at[0, g, 2 + b], recv_sem.at[0, g, b])

    def forward(side, place, g):
        return pltpu.make_async_remote_copy(
            src_ref=big.at[place, g, pl.ds(2, 2)],
            dst_ref=big.at[place, g, pl.ds(4 * side, 2)],
            send_sem=fsend_sem.at[side, place, g],
            recv_sem=frecv_sem.at[side, place, g],
            device_id=(t, left if side else right),
            device_id_type=MESH,
        )

    lane_group = lax.broadcasted_iota(jnp.int32, (CB, LANES), 1) // BINS
    low_half = lane_group < 2
    even_part = lane_group % 2 == 0

    def transform(step, carry):
        g = step // 2
        b = step % 2

        @pl.when(step == 2 * (GROUPS - 1))
        def _():
            halo.wait()

            @pl.when(t == RUNS - 1)
            def _():
                xh[:, pl.ds(samples, HALF)] = jnp.zeros((2 * CB, HALF), jnp.bfloat16)

        rows = pl.ds(pl.multiple_of(b * CB, CB), CB)
        frames = jnp.concatenate(
            [
                xh[rows, pl.ds(pl.multiple_of(g * (JG * HALF) + jj * HALF, HALF), SEG)]
                for jj in range(JG)
            ],
            axis=0,
        )
        spec[...] = jnp.dot(frames, tab[...], preferred_element_type=jnp.float32)
        for jj in range(JG):
            part = pl.ds(jj * CB, CB)
            real = spec[part, pl.ds(0, NF)]
            imag = spec[part, pl.ds(NF, NF)]
            power = real * real + imag * imag
            head = power.astype(jnp.bfloat16)
            rest = (power - head.astype(jnp.float32)).astype(jnp.bfloat16)
            total = jnp.dot(head, ban[...], preferred_element_type=jnp.float32)
            total += jnp.dot(rest, ban[...], preferred_element_type=jnp.float32)
            scale = lax.rsqrt(total * inv[0:1, :] + whiten_eps)
            spec[part, pl.ds(0, NF)] = real * scale
            spec[part, pl.ds(NF, NF)] = imag * scale
        for q in range(2):
            for h in range(2):
                column = pl.ds(q * NF + h * LANES, LANES)
                tiles = [spec[pl.ds(jj * CB, CB), column] for jj in range(JG)]

                def swap(a, c, mask, by):
                    return (
                        jnp.where(mask, a, pltpu.roll(c, by, 1)),
                        jnp.where(mask, pltpu.roll(a, LANES - by, 1), c),
                    )

                t0, t2 = swap(tiles[0], tiles[2], low_half, 2 * BINS)
                t1, t3 = swap(tiles[1], tiles[3], low_half, 2 * BINS)
                u0, u1 = swap(t0, t1, even_part, BINS)
                u2, u3 = swap(t2, t3, even_part, BINS)
                for s, tile in enumerate((u0, u1, u2, u3)):
                    send[h * 4 + s, g, b, q] = tile.astype(jnp.bfloat16)
        own_copy(g, b).start()
        for place in range(1, RUNS):
            run_copy(place, g, b).start()
        return carry

    lax.fori_loop(0, 2 * GROUPS, transform, 0)

    base = edges[0, 0]
    bin_ids = lax.broadcasted_iota(jnp.int32, (CB, LANES), 1) % BINS
    for k in range(BANDS_DEV):
        inside = (bin_ids >= edges[k, 0] - base) & (bin_ids < edges[k, 1] - base)
        masks[k] = inside.astype(jnp.float32).astype(jnp.bfloat16)
    acc[...] = jnp.zeros_like(acc)

    def receive(step):
        g = step // 2
        for half in range(2):
            @pl.when(step % 2 == half)
            def _():
                for place in range(4 * half, 4 * half + 4):
                    for b in range(2):
                        if place == 0:
                            own_copy(g, b).wait()
                        else:
                            run_copy(place, g, b).wait_recv()
                    forward(0, place, g).start()
                    forward(1, place, g).start()

    def multiply(step):
        g = step // 2
        first = (step % 2) * 4
        for side in range(2):
            for i in range(4):
                forward(side, first + i, g).wait_recv()

        def one_left(i, carry):
            side = i // 4
            block = i - 2 * side
            base_right = 2 + 2 * side
            rights = jnp.concatenate(
                [
                    jnp.concatenate(
                        [big[first + p, g, base_right + n, q] for p in range(4) for q in range(2)],
                        axis=1,
                    )
                    for n in range(2)
                ],
                axis=0,
            )
            for k in range(BANDS_DEV):
                mask = masks[k]
                pieces_re = []
                pieces_im = []
                for p in range(4):
                    l0 = big[first + p, g, block, 0] * mask
                    l1 = big[first + p, g, block, 1] * mask
                    pieces_re += [l0, l1]
                    pieces_im += [l1, -l0]
                both = jnp.concatenate(
                    [jnp.concatenate(pieces_re, axis=1), jnp.concatenate(pieces_im, axis=1)], axis=0
                )
                sums = lax.dot_general(
                    both, rights, (((1,), (1,)), ((), ())), preferred_element_type=jnp.float32
                )
                for n in range(2):
                    for q in range(2):
                        acc[2 * i + n, k, q] += sums[q * CB:(q + 1) * CB, n * CB:(n + 1) * CB]
            return carry

        lax.fori_loop(0, 6, one_left, 0)

    receive(0)

    def steps(step, carry):
        receive(step)
        multiply(step - 1)
        return carry

    lax.fori_loop(1, 2 * GROUPS, steps, 0)
    multiply(2 * GROUPS - 1)

    first_block = 2 * ch - 2
    scales = []
    for k in range(BANDS_DEV):
        width = jnp.full((8, LANES), edges[k, 1] - edges[k, 0], jnp.int32).astype(jnp.float32)
        scales.append((1.0 / jnp.sqrt(128.0 * width))[0:1, :])
    for r in range(ROWS):
        a = slots[r, 0]
        l = jnp.clip(a - first_block, 0, 3)
        n = jnp.clip(slots[r, 1] - first_block, 2, 5)
        far = n >= 4
        index = jnp.clip(jnp.where(far, 2 * (l + 2) + n - 4, 2 * l + n - 2), 0, 11)
        live = a >= 0
        for k in range(BANDS_DEV):
            for q in range(2):
                value = acc[index, k, q] * scales[k]
                stage[r, k, q] = jnp.where(live, value, 0.0)
        pltpu.make_async_copy(stage.at[r], out.at[r], out_sem.at[r]).start()

    def drain(step, carry):
        g = step // 2
        b = step % 2
        for place in range(1, RUNS):
            run_copy(place, g, b).wait_send()
        return carry

    lax.fori_loop(0, 2 * GROUPS, drain, 0)

    def drain_forward(g, carry):
        for place in range(RUNS):
            forward(0, place, g).wait_send()
            forward(1, place, g).wait_send()
        return carry

    lax.fori_loop(0, GROUPS, drain_forward, 0)
    for r in range(ROWS):
        pltpu.make_async_copy(stage.at[r], out.at[r], out_sem.at[r]).wait()


def shards(traces, band_edges, slot_pairs):
    tables, near, inverse = constant_tables()
    smem = pl.BlockSpec(memory_space=pltpu.SMEM)
    hbm = pl.BlockSpec(memory_space=pl.ANY)
    bf16 = jnp.bfloat16
    return pl.pallas_call(
        kernel,
        out_shape=jax.ShapeDtypeStruct((ROWS, BANDS_DEV, 2, CB, CB), jnp.float32),
        in_specs=[smem, smem, hbm, hbm, hbm, hbm],
        out_specs=hbm,
        scratch_shapes=[
            pltpu.VMEM((2 * CB, 4096 + HALF), bf16),
            pltpu.VMEM((SEG, 2 * NF), bf16),
            pltpu.VMEM((NF, NF), bf16),
            pltpu.VMEM((8, NF), jnp.float32),
            pltpu.VMEM((JG * CB, 2 * NF), jnp.float32),
            pltpu.VMEM((RUNS, GROUPS, 2, 2, CB, LANES), bf16),
            pltpu.VMEM((RUNS, GROUPS, 6, 2, CB, LANES), bf16),
            pltpu.VMEM((12, BANDS_DEV, 2, CB, CB), jnp.float32),
            pltpu.VMEM((BANDS_DEV, CB, LANES), bf16),
            pltpu.VMEM((ROWS, BANDS_DEV, 2, CB, CB), jnp.float32),
            pltpu.SemaphoreType.DMA((4,)),
            pltpu.SemaphoreType.DMA((2,)),
            pltpu.SemaphoreType.DMA((ROWS,)),
            pltpu.SemaphoreType.DMA((RUNS, GROUPS, 2)),
            pltpu.SemaphoreType.DMA((RUNS, GROUPS, 2)),
            pltpu.SemaphoreType.DMA((2, RUNS, GROUPS)),
            pltpu.SemaphoreType.DMA((2, RUNS, GROUPS)),
        ],
        compiler_params=pltpu.CompilerParams(
            collective_id=0, has_side_effects=True, vmem_limit_bytes=56 * 2**20
        ),
        name="cross_spectra",
    )(band_edges, slot_pairs, traces, tables, near, inverse)


def solution(mesh):
    in_specs = (P("chan", "tm"), P("tm", None), P("chan", None))
    out_specs = P("chan", "tm", None, None, None)
    return jax.shard_map(shards, mesh=mesh, in_specs=in_specs, out_specs=out_specs, check_vma=False)
```

```python
import functools

import jax
import jax.numpy as jnp
import numpy as np
from jax import lax
from jax.experimental import pallas as pl
from jax.experimental.pallas import tpu as pltpu
from jax.sharding import PartitionSpec as P

CB = 128
SEG = 512
HALF = 256
NF = 256
SMOOTH = 64
LANES = 128
RUNS = 8
BINS = 32
GROUPS = 4
JG = 4
BANDS_DEV = 4
ROWS = 10
HOPS = (0, 4, 3, 5, 2, 6, 1, 7)
PAIRS = 4
UNITS = GROUPS * PAIRS
AHEAD = 3
LATER = 3

whiten_eps = 1e-06
MESH = pl.DeviceIdType.MESH


def constant_tables():
    n = np.arange(SEG)[:, None].astype(np.int64)
    f = np.arange(NF)[None, :].astype(np.int64)
    phase = (n * f % SEG).astype(np.float64) * (2.0 * np.pi / SEG)
    taper = 0.5 - 0.5 * np.cos(np.arange(SEG).astype(np.float64) * (2.0 * np.pi / SEG))
    tables = np.concatenate([taper[:, None] * np.cos(phase), -taper[:, None] * np.sin(phase)], axis=1)
    bins = np.arange(NF)
    near = (np.abs(bins[:, None] - bins[None, :]) <= SMOOTH).astype(np.float32)
    return (
        jnp.asarray(tables.astype(np.float32), jnp.bfloat16),
        jnp.asarray(near, jnp.bfloat16),
    )


def cross_kernel(
    edges_hbm, traces, tables, near, acc,
    edges, xh, tab, ban, spec, send, big, masks,
    load_sem, halo_sem, send_sem, recv_sem, fsend_sem, frecv_sem,
):
    t = lax.axis_index("tm")
    ch = lax.axis_index("chan")
    chans = 32
    samples = 4096
    early = (JG + 1) * HALF

    loads = [
        pltpu.make_async_copy(tables, tab, load_sem.at[0]),
        pltpu.make_async_copy(
            traces.at[:, pl.ds(0, early)], xh.at[:, pl.ds(0, early)], load_sem.at[1]
        ),
        pltpu.make_async_copy(near, ban, load_sem.at[2]),
        pltpu.make_async_copy(
            traces.at[:, pl.ds(early, samples - early)],
            xh.at[:, pl.ds(early, samples - early)],
            load_sem.at[3],
        ),
        pltpu.make_async_copy(edges_hbm, edges, load_sem.at[4]),
    ]
    for load in loads:
        load.start()

    def tm_at(step):
        return lax.rem(t + step, RUNS)

    right = lax.rem(ch + 1, chans)
    left = lax.rem(ch + chans - 1, chans)

    barrier = pltpu.get_barrier_semaphore()
    for hop in range(1, RUNS):
        pl.semaphore_signal(barrier, inc=1, device_id=(tm_at(hop), ch), device_id_type=MESH)
    pl.semaphore_signal(barrier, inc=1, device_id=(t, right), device_id_type=MESH)
    pl.semaphore_signal(barrier, inc=1, device_id=(t, left), device_id_type=MESH)

    halo = pltpu.make_async_remote_copy(
        src_ref=traces.at[:, pl.ds(0, HALF)],
        dst_ref=xh.at[:, pl.ds(samples, HALF)],
        send_sem=halo_sem.at[0],
        recv_sem=halo_sem.at[1],
        device_id=(tm_at(RUNS - 1), ch),
        device_id_type=MESH,
    )

    def run_copy(place, g, b):
        run = tm_at(HOPS[place])
        return pltpu.make_async_remote_copy(
            src_ref=send.at[run, g, b],
            dst_ref=big.at[place, g, 2 + b],
            send_sem=send_sem.at[place, g, b],
            recv_sem=recv_sem.at[place, g, b],
            device_id=(run, ch),
            device_id_type=MESH,
        )

    def own_copy(g, b):
        return pltpu.make_async_copy(send.at[t, g, b], big.at[0, g, 2 + b], recv_sem.at[0, g, b])

    def forward(side, place, g, b):
        return pltpu.make_async_remote_copy(
            src_ref=big.at[place, g, 2 + b],
            dst_ref=big.at[place, g, 4 * side + b],
            send_sem=fsend_sem.at[side, place, g, b],
            recv_sem=frecv_sem.at[side, place, g, b],
            device_id=(t, left if side else right),
            device_id_type=MESH,
        )

    lane = lax.broadcasted_iota(jnp.int32, (CB, LANES), 1)
    lane_group = lane // BINS
    low_half = lane_group < 2
    even_part = lane_group % 2 == 0
    bin_row = lax.broadcasted_iota(jnp.int32, (1, NF), 1)
    count = jnp.minimum(bin_row + SMOOTH + 1, NF) - jnp.maximum(bin_row - SMOOTH, 0)
    inverse = 1.0 / count.astype(jnp.float32)

    def transform(g, b):
        rows = pl.ds(pl.multiple_of(b * CB, CB), CB)
        frames = jnp.concatenate(
            [
                xh[rows, pl.ds(pl.multiple_of(g * (JG * HALF) + jj * HALF, HALF), SEG)]
                for jj in range(JG)
            ],
            axis=0,
        )
        spec[...] = jnp.dot(frames, tab[...], preferred_element_type=jnp.float32)
        for jj in range(JG):
            part = pl.ds(jj * CB, CB)
            real = spec[part, pl.ds(0, NF)]
            imag = spec[part, pl.ds(NF, NF)]
            power = real * real + imag * imag
            head = power.astype(jnp.bfloat16)
            rest = (power - head.astype(jnp.float32)).astype(jnp.bfloat16)
            total = jnp.dot(head, ban[...], preferred_element_type=jnp.float32)
            total += jnp.dot(rest, ban[...], preferred_element_type=jnp.float32)
            scale = lax.rsqrt(total * inverse + whiten_eps)
            spec[part, pl.ds(0, NF)] = real * scale
            spec[part, pl.ds(NF, NF)] = imag * scale
        for q in range(2):
            for h in range(2):
                column = pl.ds(q * NF + h * LANES, LANES)
                tiles = [spec[pl.ds(jj * CB, CB), column] for jj in range(JG)]

                def swap(a, c, mask, by):
                    return (
                        jnp.where(mask, a, pltpu.roll(c, by, 1)),
                        jnp.where(mask, pltpu.roll(a, LANES - by, 1), c),
                    )

                t0, t2 = swap(tiles[0], tiles[2], low_half, 2 * BINS)
                t1, t3 = swap(tiles[1], tiles[3], low_half, 2 * BINS)
                u0, u1 = swap(t0, t1, even_part, BINS)
                u2, u3 = swap(t2, t3, even_part, BINS)
                for s, tile in enumerate((u0, u1, u2, u3)):
                    send[h * 4 + s, g, b, q] = tile.astype(jnp.bfloat16)

    def both_blocks(g):
        def block(b, carry):
            transform(g, b)
            return carry

        lax.fori_loop(0, 2, block, 0)

    def places(pair):
        return (2 * pair, 2 * pair + 1)

    def send_unit(unit):
        g = unit // PAIRS
        for pair in range(PAIRS):
            @pl.when(unit % PAIRS == pair)
            def _():
                for b in range(2):
                    for place in places(pair):
                        if place:
                            run_copy(place, g, b).start()

    for load in loads[:3]:
        load.wait()
    both_blocks(0)
    pl.semaphore_wait(barrier, RUNS + 1)
    halo.start()
    for unit in range(AHEAD):
        send_unit(jnp.int32(unit))
    for b in range(2):
        own_copy(0, b).start()
    loads[3].wait()
    loads[4].wait()

    def later_group(g, carry):
        @pl.when(g == GROUPS - 1)
        def _():
            halo.wait()

            @pl.when(t == RUNS - 1)
            def _():
                xh[:, pl.ds(samples, HALF)] = jnp.zeros((2 * CB, HALF), jnp.bfloat16)

        both_blocks(g)
        for b in range(2):
            own_copy(g, b).start()
        return carry

    lax.fori_loop(1, GROUPS, later_group, 0)

    base = edges[0, 0]
    bin_ids = lane % BINS
    for k in range(BANDS_DEV):
        inside = (bin_ids >= edges[0, k] - base) & (bin_ids < edges[1, k] - base)
        masks[k] = inside.astype(jnp.float32).astype(jnp.bfloat16)
    acc[...] = jnp.zeros_like(acc)

    def receive(unit):
        g = unit // PAIRS
        for pair in range(PAIRS):
            @pl.when(unit % PAIRS == pair)
            def _():
                for b in range(2):
                    for place in places(pair):
                        if place == 0:
                            own_copy(g, b).wait()
                        else:
                            run_copy(place, g, b).wait_recv()
                        forward(0, place, g, b).start()
                        forward(1, place, g, b).start()

        @pl.when(unit + AHEAD < UNITS)
        def _():
            send_unit(unit + AHEAD)

    def wait_neighbours(unit):
        g = unit // PAIRS
        first = 2 * (unit % PAIRS)
        for b in range(2):
            for i in range(2):
                for side in range(2):
                    forward(side, first + i, g, b).wait_recv()

    def multiply(unit, count, place_of):
        g = unit // PAIRS
        first = 2 * (unit % PAIRS)

        def one_left(item, carry):
            i = place_of(item)
            side = i // 4
            block = i - 2 * side
            base_right = 2 + 2 * side
            rights = jnp.concatenate(
                [
                    jnp.concatenate(
                        [big[first + p, g, base_right + n, q] for p in range(2) for q in range(2)],
                        axis=1,
                    )
                    for n in range(2)
                ],
                axis=0,
            )
            for k in range(BANDS_DEV):
                mask = masks[k]
                pieces_re = []
                pieces_im = []
                for p in range(2):
                    l0 = big[first + p, g, block, 0] * mask
                    l1 = big[first + p, g, block, 1] * mask
                    pieces_re += [l0, l1]
                    pieces_im += [l1, -l0]
                both = jnp.concatenate(
                    [jnp.concatenate(pieces_re, axis=1), jnp.concatenate(pieces_im, axis=1)], axis=0
                )
                sums = lax.dot_general(
                    both, rights, (((1,), (1,)), ((), ())), preferred_element_type=jnp.float32
                )
                for n in range(2):
                    for q in range(2):
                        acc[2 * i + n, k, q] += sums[q * CB:(q + 1) * CB, n * CB:(n + 1) * CB]
            return carry

        lax.fori_loop(0, count, one_left, 0)

    def multiply_own(unit):
        multiply(unit, 2, lambda item: item + 2)

    def multiply_neighbours(unit):
        wait_neighbours(unit)
        multiply(unit, 4, lambda item: item + 2 * (item // 2))

    def drain(unit):
        g = unit // PAIRS
        for pair in range(PAIRS):
            @pl.when(unit % PAIRS == pair)
            def _():
                for place in places(pair):
                    for b in range(2):
                        if place:
                            run_copy(place, g, b).wait_send()
                        forward(0, place, g, b).wait_send()
                        forward(1, place, g, b).wait_send()

    def steps(unit, carry):
        receive(unit)
        multiply_own(unit)

        @pl.when(unit >= 1)
        def _():
            multiply_neighbours(unit - 1)

        @pl.when(unit >= LATER)
        def _():
            drain(unit - LATER)

        return carry

    lax.fori_loop(0, UNITS, steps, 0)
    multiply_neighbours(UNITS - 1)

    def drain_last(unit, carry):
        drain(unit)
        return carry

    lax.fori_loop(UNITS - LATER, UNITS, drain_last, 0)


def rows_kernel(edges, slots, acc, out, stage, out_sem):
    first_block = 2 * lax.axis_index("chan") - 2
    scales = []
    for k in range(BANDS_DEV):
        width = jnp.full((1, LANES), edges[1, k] - edges[0, k], jnp.int32).astype(jnp.float32)
        scales.append(1.0 / jnp.sqrt(128.0 * width))

    def row_copy(r):
        return pltpu.make_async_copy(stage.at[r], out.at[r], out_sem.at[r])

    def one_row(r, carry):
        a = slots[0, r]
        l = jnp.clip(a - first_block, 0, 3)
        n = jnp.clip(slots[1, r] - first_block, 2, 5)
        index = jnp.clip(jnp.where(n >= 4, 2 * (l + 2) + n - 4, 2 * l + n - 2), 0, 11)
        live = a >= 0
        for k in range(BANDS_DEV):
            for q in range(2):
                stage[r, k, q] = jnp.where(live, acc[index, k, q] * scales[k], 0.0)
        row_copy(r).start()
        return carry

    lax.fori_loop(0, ROWS, one_row, 0)
    for r in range(ROWS):
        row_copy(r).wait()


def shards(traces, band_edges, slot_pairs):
    tables, near = constant_tables()
    edges, slots = band_edges.T, slot_pairs.T
    smem = pl.BlockSpec(memory_space=pltpu.SMEM)
    vmem = pl.BlockSpec(memory_space=pltpu.VMEM)
    hbm = pl.BlockSpec(memory_space=pltpu.HBM)
    anywhere = pl.BlockSpec(memory_space=pl.ANY)
    bf16 = jnp.bfloat16
    traces = pltpu.with_memory_space_constraint(traces, pltpu.HBM)
    sums_shape = (12, BANDS_DEV, 2, CB, CB)
    sums = pl.pallas_call(
        cross_kernel,
        out_shape=pltpu.VMEM(sums_shape, jnp.float32),
        in_specs=[hbm, hbm, anywhere, anywhere],
        out_specs=vmem,
        scratch_shapes=[
            pltpu.SMEM((2, BANDS_DEV), jnp.int32),
            pltpu.VMEM((2 * CB, 4096 + HALF), bf16),
            pltpu.VMEM((SEG, 2 * NF), bf16),
            pltpu.VMEM((NF, NF), bf16),
            pltpu.VMEM((JG * CB, 2 * NF), jnp.float32),
            pltpu.VMEM((RUNS, GROUPS, 2, 2, CB, LANES), bf16),
            pltpu.VMEM((RUNS, GROUPS, 6, 2, CB, LANES), bf16),
            pltpu.VMEM((BANDS_DEV, CB, LANES), bf16),
            pltpu.SemaphoreType.DMA((5,)),
            pltpu.SemaphoreType.DMA((2,)),
            pltpu.SemaphoreType.DMA((RUNS, GROUPS, 2)),
            pltpu.SemaphoreType.DMA((RUNS, GROUPS, 2)),
            pltpu.SemaphoreType.DMA((2, RUNS, GROUPS, 2)),
            pltpu.SemaphoreType.DMA((2, RUNS, GROUPS, 2)),
        ],
        compiler_params=pltpu.CompilerParams(
            collective_id=0, has_side_effects=True, vmem_limit_bytes=56 * 2**20
        ),
        name="cross_spectra",
    )(pltpu.with_memory_space_constraint(edges, pltpu.HBM), traces, tables, near)
    sums = pltpu.with_memory_space_constraint(sums, pltpu.VMEM)
    return pl.pallas_call(
        rows_kernel,
        out_shape=jax.ShapeDtypeStruct((ROWS, BANDS_DEV, 2, CB, CB), jnp.float32),
        in_specs=[smem, smem, vmem],
        out_specs=anywhere,
        scratch_shapes=[
            pltpu.VMEM((ROWS, BANDS_DEV, 2, CB, CB), jnp.float32),
            pltpu.SemaphoreType.DMA((ROWS,)),
        ],
        compiler_params=pltpu.CompilerParams(vmem_limit_bytes=16 * 2**20),
        name="output_rows",
    )(edges, slots, sums)


def solution(mesh):
    in_specs = (P("chan", "tm"), P("tm", None), P("chan", None))
    out_specs = P("chan", "tm", None, None, None)
    return jax.shard_map(shards, mesh=mesh, in_specs=in_specs, out_specs=out_specs, check_vma=False)
```

```python
import functools

import jax
import jax.numpy as jnp
import numpy as np
from jax import lax
from jax.experimental import pallas as pl
from jax.experimental.pallas import tpu as pltpu
from jax.sharding import PartitionSpec as P

CB = 128
SEG = 512
HALF = 256
NF = 256
SMOOTH = 64
LANES = 128
RUNS = 8
BINS = 32
GROUPS = 4
JG = 4
BANDS_DEV = 4
ROWS = 10
SLOTS = RUNS * GROUPS
PAIRED = SLOTS - GROUPS
AHEAD = 16
LATER = 6

whiten_eps = 1e-06
MESH = pl.DeviceIdType.MESH


def constant_tables():
    n = np.arange(SEG)[:, None].astype(np.int64)
    f = np.arange(NF)[None, :].astype(np.int64)
    phase = (n * f % SEG).astype(np.float64) * (2.0 * np.pi / SEG)
    taper = 0.5 - 0.5 * np.cos(np.arange(SEG).astype(np.float64) * (2.0 * np.pi / SEG))
    tables = np.concatenate([taper[:, None] * np.cos(phase), -taper[:, None] * np.sin(phase)], axis=1)
    bins = np.arange(NF)
    near = (np.abs(bins[:, None] - bins[None, :]) <= SMOOTH).astype(np.float32)
    return (
        jnp.asarray(tables.astype(np.float32), jnp.bfloat16),
        jnp.asarray(near, jnp.bfloat16),
    )


def cross_kernel(
    edges_hbm, traces, tables, near, acc,
    edges, xh, tab, ban, spec, send, big, masks,
    load_sem, halo_sem, send_sem, recv_sem, fsend_sem, frecv_sem,
):
    t = lax.axis_index("tm")
    ch = lax.axis_index("chan")
    chans = 32
    samples = 4096
    early = (JG + 1) * HALF

    loads = [
        pltpu.make_async_copy(tables, tab, load_sem.at[0]),
        pltpu.make_async_copy(
            traces.at[:, pl.ds(0, early)], xh.at[:, pl.ds(0, early)], load_sem.at[1]
        ),
        pltpu.make_async_copy(near, ban, load_sem.at[2]),
        pltpu.make_async_copy(
            traces.at[:, pl.ds(early, samples - early)],
            xh.at[:, pl.ds(early, samples - early)],
            load_sem.at[3],
        ),
        pltpu.make_async_copy(edges_hbm, edges, load_sem.at[4]),
    ]
    for load in loads:
        load.start()

    def tm_at(step):
        return lax.rem(t + step, RUNS)

    right = lax.rem(ch + 1, chans)
    left = lax.rem(ch + chans - 1, chans)

    barrier = pltpu.get_barrier_semaphore()
    for hop in range(1, RUNS):
        pl.semaphore_signal(barrier, inc=1, device_id=(tm_at(hop), ch), device_id_type=MESH)
    pl.semaphore_signal(barrier, inc=1, device_id=(t, right), device_id_type=MESH)
    pl.semaphore_signal(barrier, inc=1, device_id=(t, left), device_id_type=MESH)

    halo = pltpu.make_async_remote_copy(
        src_ref=traces.at[:, pl.ds(0, HALF)],
        dst_ref=xh.at[:, pl.ds(samples, HALF)],
        send_sem=halo_sem.at[0],
        recv_sem=halo_sem.at[1],
        device_id=(tm_at(RUNS - 1), ch),
        device_id_type=MESH,
    )

    def route(slot):
        near = (slot - GROUPS) // RUNS + 1
        place = (slot - GROUPS) % RUNS
        far = slot // PAIRED
        hop = near + (slot % 2) * (RUNS - 2 * near)
        return tm_at(hop), far * place + (1 - far) * (place // 2)

    def run_copy(slot, b):
        run, g = route(slot)
        return pltpu.make_async_remote_copy(
            src_ref=send.at[run, g, b],
            dst_ref=big.at[slot, 2 + b],
            send_sem=send_sem.at[slot, b],
            recv_sem=recv_sem.at[slot, b],
            device_id=(run, ch),
            device_id_type=MESH,
        )

    def own_copy(g, b):
        return pltpu.make_async_copy(send.at[t, g, b], big.at[g, 2 + b], recv_sem.at[g, b])

    def forward(side, slot, b):
        return pltpu.make_async_remote_copy(
            src_ref=big.at[slot, 2 + b],
            dst_ref=big.at[slot, 4 * side + b],
            send_sem=fsend_sem.at[side, slot, b],
            recv_sem=frecv_sem.at[side, slot, b],
            device_id=(t, left if side else right),
            device_id_type=MESH,
        )

    lane = lax.broadcasted_iota(jnp.int32, (CB, LANES), 1)
    lane_group = lane // BINS
    low_half = lane_group < 2
    even_part = lane_group % 2 == 0
    bin_row = lax.broadcasted_iota(jnp.int32, (1, NF), 1)
    count = jnp.minimum(bin_row + SMOOTH + 1, NF) - jnp.maximum(bin_row - SMOOTH, 0)
    inverse = 1.0 / count.astype(jnp.float32)

    def transform(g, b):
        rows = pl.ds(pl.multiple_of(b * CB, CB), CB)
        frames = jnp.concatenate(
            [
                xh[rows, pl.ds(pl.multiple_of(g * (JG * HALF) + jj * HALF, HALF), SEG)]
                for jj in range(JG)
            ],
            axis=0,
        )
        spec[...] = jnp.dot(frames, tab[...], preferred_element_type=jnp.float32)
        for jj in range(JG):
            part = pl.ds(jj * CB, CB)
            real = spec[part, pl.ds(0, NF)]
            imag = spec[part, pl.ds(NF, NF)]
            power = real * real + imag * imag
            head = power.astype(jnp.bfloat16)
            rest = (power - head.astype(jnp.float32)).astype(jnp.bfloat16)
            total = jnp.dot(head, ban[...], preferred_element_type=jnp.float32)
            total += jnp.dot(rest, ban[...], preferred_element_type=jnp.float32)
            scale = lax.rsqrt(total * inverse + whiten_eps)
            spec[part, pl.ds(0, NF)] = real * scale
            spec[part, pl.ds(NF, NF)] = imag * scale
        for q in range(2):
            for h in range(2):
                column = pl.ds(q * NF + h * LANES, LANES)
                tiles = [spec[pl.ds(jj * CB, CB), column] for jj in range(JG)]

                def swap(a, c, mask, by):
                    return (
                        jnp.where(mask, a, pltpu.roll(c, by, 1)),
                        jnp.where(mask, pltpu.roll(a, LANES - by, 1), c),
                    )

                t0, t2 = swap(tiles[0], tiles[2], low_half, 2 * BINS)
                t1, t3 = swap(tiles[1], tiles[3], low_half, 2 * BINS)
                u0, u1 = swap(t0, t1, even_part, BINS)
                u2, u3 = swap(t2, t3, even_part, BINS)
                for s, tile in enumerate((u0, u1, u2, u3)):
                    send[h * 4 + s, g, b, q] = tile.astype(jnp.bfloat16)

    def both_blocks(g):
        def block(b, carry):
            transform(g, b)
            return carry

        lax.fori_loop(0, 2, block, 0)

    def send_slot(slot):
        for b in range(2):
            run_copy(slot, b).start()

    def send_nearest(g):
        for b in range(2):
            own_copy(g, b).start()
        for i in range(2):
            send_slot(GROUPS + 2 * g + i)

    for load in loads[:3]:
        load.wait()
    both_blocks(0)
    pl.semaphore_wait(barrier, RUNS + 1)
    halo.start()
    send_nearest(jnp.int32(0))
    loads[3].wait()
    loads[4].wait()

    def later_group(g, carry):
        @pl.when(g == GROUPS - 1)
        def _():
            halo.wait()

            @pl.when(t == RUNS - 1)
            def _():
                xh[:, pl.ds(samples, HALF)] = jnp.zeros((2 * CB, HALF), jnp.bfloat16)

        both_blocks(g)
        send_nearest(g)
        return carry

    lax.fori_loop(1, GROUPS, later_group, 0)

    def send_more(slot, carry):
        send_slot(slot)
        return carry

    lax.fori_loop(3 * GROUPS, AHEAD, send_more, 0)

    base = edges[0, 0]
    bin_ids = lane % BINS
    for k in range(BANDS_DEV):
        inside = (bin_ids >= edges[0, k] - base) & (bin_ids < edges[1, k] - base)
        masks[k] = inside.astype(jnp.float32).astype(jnp.bfloat16)
    acc[...] = jnp.zeros_like(acc)

    def receive(slot):
        for b in range(2):
            run_copy(slot, b).wait_recv()
            forward(0, slot, b).start()
            forward(1, slot, b).start()

    def receive_own(g):
        for b in range(2):
            own_copy(g, b).wait()
            forward(0, g, b).start()
            forward(1, g, b).start()

    def wait_neighbours(first, depth):
        for b in range(2):
            for i in range(depth):
                for side in range(2):
                    forward(side, first + i, b).wait_recv()

    def multiply(first, depth, count, place_of):
        def one_left(item, carry):
            i = place_of(item)
            side = i // 4
            block = i - 2 * side
            base_right = 2 + 2 * side
            rights = jnp.concatenate(
                [
                    jnp.concatenate(
                        [big[first + p, base_right + n, q] for p in range(depth) for q in range(2)],
                        axis=1,
                    )
                    for n in range(2)
                ],
                axis=0,
            )
            for k in range(BANDS_DEV):
                mask = masks[k]
                pieces_re = []
                pieces_im = []
                for p in range(depth):
                    l0 = big[first + p, block, 0] * mask
                    l1 = big[first + p, block, 1] * mask
                    pieces_re += [l0, l1]
                    pieces_im += [l1, -l0]
                both = jnp.concatenate(
                    [jnp.concatenate(pieces_re, axis=1), jnp.concatenate(pieces_im, axis=1)], axis=0
                )
                sums = lax.dot_general(
                    both, rights, (((1,), (1,)), ((), ())), preferred_element_type=jnp.float32
                )
                for n in range(2):
                    for q in range(2):
                        acc[2 * i + n, k, q] += sums[q * CB:(q + 1) * CB, n * CB:(n + 1) * CB]
            return carry

        lax.fori_loop(0, count, one_left, 0)

    def multiply_own(first, depth):
        multiply(first, depth, 2, lambda item: item + 2)

    def multiply_neighbours(first, depth):
        wait_neighbours(first, depth)
        multiply(first, depth, 4, lambda item: item + 2 * (item // 2))

    def drain(slot, carry):
        for b in range(2):
            @pl.when(slot >= GROUPS)
            def _():
                run_copy(slot, b).wait_send()

            forward(0, slot, b).wait_send()
            forward(1, slot, b).wait_send()
        return carry

    def paired_step(unit, carry):
        first = 2 * unit
        for i in range(2):
            @pl.when(unit < GROUPS // 2)
            def _():
                receive_own(first + i)

            @pl.when(unit >= GROUPS // 2)
            def _():
                receive(first + i)

        @pl.when(first + AHEAD < SLOTS)
        def _():
            for i in range(2):
                send_slot(first + AHEAD + i)

        multiply_own(first, 2)

        @pl.when(unit >= 1)
        def _():
            multiply_neighbours(first - 2, 2)

        @pl.when(first >= LATER)
        def _():
            for i in range(2):
                drain(first - LATER + i, 0)

        return carry

    lax.fori_loop(0, PAIRED // 2, paired_step, 0)
    receive(jnp.int32(PAIRED))
    multiply_own(PAIRED, 1)
    multiply_neighbours(PAIRED - 2, 2)

    def far_step(slot, carry):
        receive(slot)
        multiply_own(slot, 1)
        multiply_neighbours(slot - 1, 1)
        return carry

    lax.fori_loop(PAIRED + 1, SLOTS, far_step, 0)
    multiply_neighbours(SLOTS - 1, 1)
    lax.fori_loop(PAIRED - LATER, SLOTS, drain, 0)


def rows_kernel(edges, slots, acc, out, stage, out_sem):
    first_block = 2 * lax.axis_index("chan") - 2
    scales = []
    for k in range(BANDS_DEV):
        width = jnp.full((1, LANES), edges[1, k] - edges[0, k], jnp.int32).astype(jnp.float32)
        scales.append(1.0 / jnp.sqrt(128.0 * width))

    def row_copy(r):
        return pltpu.make_async_copy(stage.at[r], out.at[r], out_sem.at[r])

    def one_row(r, carry):
        a = slots[0, r]
        l = jnp.clip(a - first_block, 0, 3)
        n = jnp.clip(slots[1, r] - first_block, 2, 5)
        index = jnp.clip(jnp.where(n >= 4, 2 * (l + 2) + n - 4, 2 * l + n - 2), 0, 11)
        live = a >= 0
        for k in range(BANDS_DEV):
            for q in range(2):
                stage[r, k, q] = jnp.where(live, acc[index, k, q] * scales[k], 0.0)
        row_copy(r).start()
        return carry

    lax.fori_loop(0, ROWS, one_row, 0)
    for r in range(ROWS):
        row_copy(r).wait()


def shards(traces, band_edges, slot_pairs):
    tables, near = constant_tables()
    edges, slots = band_edges.T, slot_pairs.T
    smem = pl.BlockSpec(memory_space=pltpu.SMEM)
    vmem = pl.BlockSpec(memory_space=pltpu.VMEM)
    hbm = pl.BlockSpec(memory_space=pltpu.HBM)
    anywhere = pl.BlockSpec(memory_space=pl.ANY)
    bf16 = jnp.bfloat16
    traces = pltpu.with_memory_space_constraint(traces, pltpu.HBM)
    sums_shape = (12, BANDS_DEV, 2, CB, CB)
    sums = pl.pallas_call(
        cross_kernel,
        out_shape=pltpu.VMEM(sums_shape, jnp.float32),
        in_specs=[hbm, hbm, anywhere, anywhere],
        out_specs=vmem,
        scratch_shapes=[
            pltpu.SMEM((2, BANDS_DEV), jnp.int32),
            pltpu.VMEM((2 * CB, 4096 + HALF), bf16),
            pltpu.VMEM((SEG, 2 * NF), bf16),
            pltpu.VMEM((NF, NF), bf16),
            pltpu.VMEM((JG * CB, 2 * NF), jnp.float32),
            pltpu.VMEM((RUNS, GROUPS, 2, 2, CB, LANES), bf16),
            pltpu.VMEM((SLOTS, 6, 2, CB, LANES), bf16),
            pltpu.VMEM((BANDS_DEV, CB, LANES), bf16),
            pltpu.SemaphoreType.DMA((5,)),
            pltpu.SemaphoreType.DMA((2,)),
            pltpu.SemaphoreType.DMA((SLOTS, 2)),
            pltpu.SemaphoreType.DMA((SLOTS, 2)),
            pltpu.SemaphoreType.DMA((2, SLOTS, 2)),
            pltpu.SemaphoreType.DMA((2, SLOTS, 2)),
        ],
        compiler_params=pltpu.CompilerParams(
            collective_id=0, has_side_effects=True, vmem_limit_bytes=56 * 2**20
        ),
        name="cross_spectra",
    )(pltpu.with_memory_space_constraint(edges, pltpu.HBM), traces, tables, near)
    sums = pltpu.with_memory_space_constraint(sums, pltpu.VMEM)
    return pl.pallas_call(
        rows_kernel,
        out_shape=jax.ShapeDtypeStruct((ROWS, BANDS_DEV, 2, CB, CB), jnp.float32),
        in_specs=[smem, smem, vmem],
        out_specs=anywhere,
        scratch_shapes=[
            pltpu.VMEM((ROWS, BANDS_DEV, 2, CB, CB), jnp.float32),
            pltpu.SemaphoreType.DMA((ROWS,)),
        ],
        compiler_params=pltpu.CompilerParams(vmem_limit_bytes=16 * 2**20),
        name="output_rows",
    )(edges, slots, sums)


def solution(mesh):
    in_specs = (P("chan", "tm"), P("tm", None), P("chan", None))
    out_specs = P("chan", "tm", None, None, None)
    return jax.shard_map(shards, mesh=mesh, in_specs=in_specs, out_specs=out_specs, check_vma=False)
```

```python
import functools

import jax
import jax.numpy as jnp
import numpy as np
from jax import lax
from jax.experimental import pallas as pl
from jax.experimental.pallas import tpu as pltpu
from jax.sharding import PartitionSpec as P

CB = 128
SEG = 512
HALF = 256
NF = 256
SMOOTH = 64
LANES = 128
RUNS = 8
BINS = 32
GROUPS = 4
JG = 4
BANDS_DEV = 4
ROWS = 10
SLOTS = RUNS * GROUPS
PAIRED = SLOTS - GROUPS
FOURS = 5 * GROUPS
THREES = 6 * GROUPS
AHEAD = 10
LATER = 6

whiten_eps = 1e-06
MESH = pl.DeviceIdType.MESH


def constant_tables():
    n = np.arange(SEG)[:, None].astype(np.int64)
    f = np.arange(NF)[None, :].astype(np.int64)
    phase = (n * f % SEG).astype(np.float64) * (2.0 * np.pi / SEG)
    taper = 0.5 - 0.5 * np.cos(np.arange(SEG).astype(np.float64) * (2.0 * np.pi / SEG))
    tables = np.concatenate([taper[:, None] * np.cos(phase), -taper[:, None] * np.sin(phase)], axis=1)
    bins = np.arange(NF)
    near = (np.abs(bins[:, None] - bins[None, :]) <= SMOOTH).astype(np.float32)
    return (
        jnp.asarray(tables.astype(np.float32), jnp.bfloat16),
        jnp.asarray(near, jnp.bfloat16),
    )


def cross_kernel(
    edges_hbm, traces, tables, near, acc,
    edges, xh, tab, ban, spec, send, big, masks,
    load_sem, halo_sem, send_sem, recv_sem, fsend_sem, frecv_sem,
):
    t = lax.axis_index("tm")
    ch = lax.axis_index("chan")
    chans = 32
    samples = 4096
    early = (JG + 1) * HALF

    loads = [
        pltpu.make_async_copy(
            traces.at[pl.ds(0, CB), pl.ds(0, early)],
            xh.at[pl.ds(0, CB), pl.ds(0, early)],
            load_sem.at[0],
        ),
        pltpu.make_async_copy(tables, tab, load_sem.at[1]),
        pltpu.make_async_copy(near, ban, load_sem.at[2]),
        pltpu.make_async_copy(
            traces.at[pl.ds(CB, CB), pl.ds(0, early)],
            xh.at[pl.ds(CB, CB), pl.ds(0, early)],
            load_sem.at[5],
        ),
        pltpu.make_async_copy(
            traces.at[:, pl.ds(early, samples - early)],
            xh.at[:, pl.ds(early, samples - early)],
            load_sem.at[3],
        ),
        pltpu.make_async_copy(edges_hbm, edges, load_sem.at[4]),
    ]
    for load in loads[:4]:
        load.start()

    def tm_at(step):
        return lax.rem(t + step, RUNS)

    right = lax.rem(ch + 1, chans)
    left = lax.rem(ch + chans - 1, chans)

    barrier = pltpu.get_barrier_semaphore()
    for hop in range(1, RUNS):
        pl.semaphore_signal(barrier, inc=1, device_id=(tm_at(hop), ch), device_id_type=MESH)
    pl.semaphore_signal(barrier, inc=1, device_id=(t, right), device_id_type=MESH)
    pl.semaphore_signal(barrier, inc=1, device_id=(t, left), device_id_type=MESH)

    halo = pltpu.make_async_remote_copy(
        src_ref=traces.at[:, pl.ds(0, HALF)],
        dst_ref=xh.at[:, pl.ds(samples, HALF)],
        send_sem=halo_sem.at[0],
        recv_sem=halo_sem.at[1],
        device_id=(tm_at(RUNS - 1), ch),
        device_id_type=MESH,
    )

    def route(slot):
        place = (slot - GROUPS) % RUNS
        late = slot // THREES
        fours = slot // FOURS - late
        early = 1 - late - fours
        near = early * ((slot - GROUPS) // RUNS + 1) + 4 * fours + 3 * late
        hop = near + (slot % 2) * (RUNS - 2 * near)
        g = early * (place // 2) + fours * (slot - FOURS) + late * ((slot - THREES) // 2)
        return tm_at(hop), g

    def run_copy(slot, b):
        run, g = route(slot)
        return pltpu.make_async_remote_copy(
            src_ref=send.at[run, g, b],
            dst_ref=big.at[slot, 2 + b],
            send_sem=send_sem.at[slot, b],
            recv_sem=recv_sem.at[slot, b],
            device_id=(run, ch),
            device_id_type=MESH,
        )

    def own_copy(g, b):
        return pltpu.make_async_copy(send.at[t, g, b], big.at[g, 2 + b], recv_sem.at[g, b])

    def forward(side, slot, b):
        return pltpu.make_async_remote_copy(
            src_ref=big.at[slot, 2 + b],
            dst_ref=big.at[slot, 4 * side + b],
            send_sem=fsend_sem.at[side, slot, b],
            recv_sem=frecv_sem.at[side, slot, b],
            device_id=(t, left if side else right),
            device_id_type=MESH,
        )

    lane = lax.broadcasted_iota(jnp.int32, (CB, LANES), 1)
    lane_group = lane // BINS
    low_half = lane_group < 2
    even_part = lane_group % 2 == 0
    bin_row = lax.broadcasted_iota(jnp.int32, (1, NF), 1)
    count = jnp.minimum(bin_row + SMOOTH + 1, NF) - jnp.maximum(bin_row - SMOOTH, 0)
    inverse = 1.0 / count.astype(jnp.float32)

    def transform(g, b):
        rows = pl.ds(pl.multiple_of(b * CB, CB), CB)
        frames = jnp.concatenate(
            [
                xh[rows, pl.ds(pl.multiple_of(g * (JG * HALF) + jj * HALF, HALF), SEG)]
                for jj in range(JG)
            ],
            axis=0,
        )
        spec[...] = jnp.dot(frames, tab[...], preferred_element_type=jnp.float32)
        for jj in range(JG):
            part = pl.ds(jj * CB, CB)
            real = spec[part, pl.ds(0, NF)]
            imag = spec[part, pl.ds(NF, NF)]
            power = real * real + imag * imag
            head = power.astype(jnp.bfloat16)
            rest = (power - head.astype(jnp.float32)).astype(jnp.bfloat16)
            total = jnp.dot(head, ban[...], preferred_element_type=jnp.float32)
            total += jnp.dot(rest, ban[...], preferred_element_type=jnp.float32)
            scale = lax.rsqrt(total * inverse + whiten_eps)
            spec[part, pl.ds(0, NF)] = real * scale
            spec[part, pl.ds(NF, NF)] = imag * scale
        for q in range(2):
            for h in range(2):
                column = pl.ds(q * NF + h * LANES, LANES)
                tiles = [spec[pl.ds(jj * CB, CB), column] for jj in range(JG)]

                def swap(a, c, mask, by):
                    return (
                        jnp.where(mask, a, pltpu.roll(c, by, 1)),
                        jnp.where(mask, pltpu.roll(a, LANES - by, 1), c),
                    )

                t0, t2 = swap(tiles[0], tiles[2], low_half, 2 * BINS)
                t1, t3 = swap(tiles[1], tiles[3], low_half, 2 * BINS)
                u0, u1 = swap(t0, t1, even_part, BINS)
                u2, u3 = swap(t2, t3, even_part, BINS)
                for s, tile in enumerate((u0, u1, u2, u3)):
                    send[h * 4 + s, g, b, q] = tile.astype(jnp.bfloat16)

    def send_slot(slot):
        for b in range(2):
            run_copy(slot, b).start()

    def send_nearest(g, b):
        for i in range(2):
            run_copy(GROUPS + 2 * g + i, b).start()
        own_copy(g, b).start()

    for load in loads[:3]:
        load.wait()
    transform(jnp.int32(0), jnp.int32(0))
    for load in loads[4:]:
        load.start()
    pl.semaphore_wait(barrier, RUNS + 1)
    send_nearest(jnp.int32(0), 0)
    halo.start()
    loads[3].wait()
    transform(jnp.int32(0), jnp.int32(1))
    send_nearest(jnp.int32(0), 1)
    for load in loads[4:]:
        load.wait()

    def later_group(g, carry):
        @pl.when(g == GROUPS - 1)
        def _():
            halo.wait()

            @pl.when(t == RUNS - 1)
            def _():
                xh[:, pl.ds(samples, HALF)] = jnp.zeros((2 * CB, HALF), jnp.bfloat16)

        def block(b, inner):
            transform(g, b)
            send_nearest(g, b)
            return inner

        lax.fori_loop(0, 2, block, 0)
        return carry

    lax.fori_loop(1, GROUPS, later_group, 0)

    def send_more(slot, carry):
        send_slot(slot)
        return carry

    lax.fori_loop(3 * GROUPS, GROUPS + AHEAD, send_more, 0)

    base = edges[0, 0]
    bin_ids = lane % BINS
    for k in range(BANDS_DEV):
        inside = (bin_ids >= edges[0, k] - base) & (bin_ids < edges[1, k] - base)
        masks[k] = inside.astype(jnp.float32).astype(jnp.bfloat16)
    acc[...] = jnp.zeros_like(acc)

    def receive(slot):
        for b in range(2):
            run_copy(slot, b).wait_recv()
            forward(0, slot, b).start()
            forward(1, slot, b).start()

    def receive_own(g):
        for b in range(2):
            own_copy(g, b).wait()
            forward(0, g, b).start()
            forward(1, g, b).start()

    def wait_neighbours(first, depth):
        for b in range(2):
            for i in range(depth):
                for side in range(2):
                    forward(side, first + i, b).wait_recv()

    def multiply(first, depth, count, place_of):
        def one_left(item, carry):
            i = place_of(item)
            side = i // 4
            block = i - 2 * side
            base_right = 2 + 2 * side
            rights = jnp.concatenate(
                [
                    jnp.concatenate(
                        [big[first + p, base_right + n, q] for p in range(depth) for q in range(2)],
                        axis=1,
                    )
                    for n in range(2)
                ],
                axis=0,
            )
            for k in range(BANDS_DEV):
                mask = masks[k]
                pieces_re = []
                pieces_im = []
                for p in range(depth):
                    l0 = big[first + p, block, 0] * mask
                    l1 = big[first + p, block, 1] * mask
                    pieces_re += [l0, l1]
                    pieces_im += [l1, -l0]
                both = jnp.concatenate(
                    [jnp.concatenate(pieces_re, axis=1), jnp.concatenate(pieces_im, axis=1)], axis=0
                )
                sums = lax.dot_general(
                    both, rights, (((1,), (1,)), ((), ())), preferred_element_type=jnp.float32
                )
                for n in range(2):
                    for q in range(2):
                        acc[2 * i + n, k, q] += sums[q * CB:(q + 1) * CB, n * CB:(n + 1) * CB]
            return carry

        lax.fori_loop(0, count, one_left, 0)

    def multiply_own(first, depth):
        multiply(first, depth, 2, lambda item: item + 2)

    def multiply_neighbours(first, depth):
        wait_neighbours(first, depth)
        multiply(first, depth, 4, lambda item: item + 2 * (item // 2))

    def drain(slot, carry):
        for b in range(2):
            @pl.when(slot >= GROUPS)
            def _():
                run_copy(slot, b).wait_send()

            forward(0, slot, b).wait_send()
            forward(1, slot, b).wait_send()
        return carry

    def paired_step(unit, carry):
        first = 2 * unit
        for i in range(2):
            @pl.when(unit < GROUPS // 2)
            def _():
                receive_own(first + i)

            @pl.when(unit >= GROUPS // 2)
            def _():
                receive(first + i)

        @pl.when((first >= GROUPS) & (first + AHEAD < SLOTS))
        def _():
            for i in range(2):
                send_slot(first + AHEAD + i)

        multiply_own(first, 2)

        @pl.when(unit >= 1)
        def _():
            multiply_neighbours(first - 2, 2)

        @pl.when(first >= LATER)
        def _():
            for i in range(2):
                drain(first - LATER + i, 0)

        return carry

    lax.fori_loop(0, PAIRED // 2, paired_step, 0)
    receive(jnp.int32(PAIRED))
    multiply_own(PAIRED, 1)
    multiply_neighbours(PAIRED - 2, 2)

    def far_step(slot, carry):
        receive(slot)
        multiply_own(slot, 1)
        multiply_neighbours(slot - 1, 1)
        return carry

    lax.fori_loop(PAIRED + 1, SLOTS, far_step, 0)
    multiply_neighbours(SLOTS - 1, 1)
    lax.fori_loop(PAIRED - LATER, SLOTS, drain, 0)


def rows_kernel(edges, slots, acc, out, stage, out_sem):
    first_block = 2 * lax.axis_index("chan") - 2
    scales = []
    for k in range(BANDS_DEV):
        width = jnp.full((1, LANES), edges[1, k] - edges[0, k], jnp.int32).astype(jnp.float32)
        scales.append(1.0 / jnp.sqrt(128.0 * width))

    def row_copy(r):
        return pltpu.make_async_copy(stage.at[r], out.at[r], out_sem.at[r])

    def one_row(r, carry):
        a = slots[0, r]
        l = jnp.clip(a - first_block, 0, 3)
        n = jnp.clip(slots[1, r] - first_block, 2, 5)
        index = jnp.clip(jnp.where(n >= 4, 2 * (l + 2) + n - 4, 2 * l + n - 2), 0, 11)
        live = a >= 0
        for k in range(BANDS_DEV):
            for q in range(2):
                stage[r, k, q] = jnp.where(live, acc[index, k, q] * scales[k], 0.0)
        row_copy(r).start()
        return carry

    lax.fori_loop(0, ROWS, one_row, 0)
    for r in range(ROWS):
        row_copy(r).wait()


def shards(traces, band_edges, slot_pairs):
    tables, near = constant_tables()
    edges, slots = band_edges.T, slot_pairs.T
    smem = pl.BlockSpec(memory_space=pltpu.SMEM)
    vmem = pl.BlockSpec(memory_space=pltpu.VMEM)
    hbm = pl.BlockSpec(memory_space=pltpu.HBM)
    anywhere = pl.BlockSpec(memory_space=pl.ANY)
    bf16 = jnp.bfloat16
    traces = pltpu.with_memory_space_constraint(traces, pltpu.HBM)
    sums_shape = (12, BANDS_DEV, 2, CB, CB)
    sums = pl.pallas_call(
        cross_kernel,
        out_shape=pltpu.VMEM(sums_shape, jnp.float32),
        in_specs=[hbm, hbm, anywhere, anywhere],
        out_specs=vmem,
        scratch_shapes=[
            pltpu.SMEM((2, BANDS_DEV), jnp.int32),
            pltpu.VMEM((2 * CB, 4096 + HALF), bf16),
            pltpu.VMEM((SEG, 2 * NF), bf16),
            pltpu.VMEM((NF, NF), bf16),
            pltpu.VMEM((JG * CB, 2 * NF), jnp.float32),
            pltpu.VMEM((RUNS, GROUPS, 2, 2, CB, LANES), bf16),
            pltpu.VMEM((SLOTS, 6, 2, CB, LANES), bf16),
            pltpu.VMEM((BANDS_DEV, CB, LANES), bf16),
            pltpu.SemaphoreType.DMA((6,)),
            pltpu.SemaphoreType.DMA((2,)),
            pltpu.SemaphoreType.DMA((SLOTS, 2)),
            pltpu.SemaphoreType.DMA((SLOTS, 2)),
            pltpu.SemaphoreType.DMA((2, SLOTS, 2)),
            pltpu.SemaphoreType.DMA((2, SLOTS, 2)),
        ],
        compiler_params=pltpu.CompilerParams(
            collective_id=0, has_side_effects=True, vmem_limit_bytes=56 * 2**20
        ),
        name="cross_spectra",
    )(pltpu.with_memory_space_constraint(edges, pltpu.HBM), traces, tables, near)
    sums = pltpu.with_memory_space_constraint(sums, pltpu.VMEM)
    return pl.pallas_call(
        rows_kernel,
        out_shape=jax.ShapeDtypeStruct((ROWS, BANDS_DEV, 2, CB, CB), jnp.float32),
        in_specs=[smem, smem, vmem],
        out_specs=anywhere,
        scratch_shapes=[
            pltpu.VMEM((ROWS, BANDS_DEV, 2, CB, CB), jnp.float32),
            pltpu.SemaphoreType.DMA((ROWS,)),
        ],
        compiler_params=pltpu.CompilerParams(vmem_limit_bytes=16 * 2**20),
        name="output_rows",
    )(edges, slots, sums)


def solution(mesh):
    in_specs = (P("chan", "tm"), P("tm", None), P("chan", None))
    out_specs = P("chan", "tm", None, None, None)
    return jax.shard_map(shards, mesh=mesh, in_specs=in_specs, out_specs=out_specs, check_vma=False)
```

```python
import functools

import jax
import jax.numpy as jnp
import numpy as np
from jax import lax
from jax.experimental import pallas as pl
from jax.experimental.pallas import tpu as pltpu
from jax.sharding import PartitionSpec as P

CB = 128
SEG = 512
HALF = 256
NF = 256
SMOOTH = 64
LANES = 128
RUNS = 8
BINS = 32
GROUPS = 4
JG = 4
BANDS_DEV = 4
ROWS = 10
SLOTS = RUNS * GROUPS
PAIRED = SLOTS - GROUPS
FOURS = 5 * GROUPS
THREES = 6 * GROUPS
AHEAD = 10
LATER = 6

whiten_eps = 1e-06
MESH = pl.DeviceIdType.MESH


def constant_tables():
    n = np.arange(SEG)[:, None].astype(np.int64)
    f = np.arange(NF)[None, :].astype(np.int64)
    phase = (n * f % SEG).astype(np.float64) * (2.0 * np.pi / SEG)
    taper = 0.5 - 0.5 * np.cos(np.arange(SEG).astype(np.float64) * (2.0 * np.pi / SEG))
    tables = np.concatenate([taper[:, None] * np.cos(phase), -taper[:, None] * np.sin(phase)], axis=1)
    bins = np.arange(NF)
    near = (np.abs(bins[:, None] - bins[None, :]) <= SMOOTH).astype(np.float32)
    return (
        jnp.asarray(tables.astype(np.float32), jnp.bfloat16),
        jnp.asarray(near, jnp.bfloat16),
    )


def cross_kernel(
    edges_hbm, traces, tables, near, acc,
    edges, xh, tab, ban, spec, send, big, masks,
    load_sem, halo_sem, send_sem, recv_sem, fsend_sem, frecv_sem,
):
    t = lax.axis_index("tm")
    ch = lax.axis_index("chan")
    chans = 32
    samples = 4096
    early = (JG + 1) * HALF

    def tm_at(step):
        return lax.rem(t + step, RUNS)

    right = lax.rem(ch + 1, chans)
    left = lax.rem(ch + chans - 1, chans)

    barrier = pltpu.get_barrier_semaphore()
    for hop in range(1, RUNS):
        pl.semaphore_signal(barrier, inc=1, device_id=(tm_at(hop), ch), device_id_type=MESH)
    pl.semaphore_signal(barrier, inc=1, device_id=(t, right), device_id_type=MESH)
    pl.semaphore_signal(barrier, inc=1, device_id=(t, left), device_id_type=MESH)

    loads = [
        pltpu.make_async_copy(
            traces.at[pl.ds(0, CB), pl.ds(0, early)],
            xh.at[pl.ds(0, CB), pl.ds(0, early)],
            load_sem.at[0],
        ),
        pltpu.make_async_copy(tables, tab, load_sem.at[1]),
        pltpu.make_async_copy(near, ban, load_sem.at[2]),
        pltpu.make_async_copy(
            traces.at[pl.ds(CB, CB), pl.ds(0, early)],
            xh.at[pl.ds(CB, CB), pl.ds(0, early)],
            load_sem.at[5],
        ),
        pltpu.make_async_copy(
            traces.at[:, pl.ds(early, samples - early)],
            xh.at[:, pl.ds(early, samples - early)],
            load_sem.at[3],
        ),
        pltpu.make_async_copy(edges_hbm, edges, load_sem.at[4]),
    ]
    for load in loads[:4]:
        load.start()

    halo = pltpu.make_async_remote_copy(
        src_ref=traces.at[:, pl.ds(0, HALF)],
        dst_ref=xh.at[:, pl.ds(samples, HALF)],
        send_sem=halo_sem.at[0],
        recv_sem=halo_sem.at[1],
        device_id=(tm_at(RUNS - 1), ch),
        device_id_type=MESH,
    )

    def route(slot):
        place = (slot - GROUPS) % RUNS
        late = slot // THREES
        fours = slot // FOURS - late
        early = 1 - late - fours
        near = early * ((slot - GROUPS) // RUNS + 1) + 4 * fours + 3 * late
        hop = near + (slot % 2) * (RUNS - 2 * near)
        g = early * (place // 2) + fours * (slot - FOURS) + late * ((slot - THREES) // 2)
        return tm_at(hop), g

    def run_copy(slot, b):
        run, g = route(slot)
        return pltpu.make_async_remote_copy(
            src_ref=send.at[run, g, b],
            dst_ref=big.at[slot, 2 + b],
            send_sem=send_sem.at[slot, b],
            recv_sem=recv_sem.at[slot, b],
            device_id=(run, ch),
            device_id_type=MESH,
        )

    def own_copy(g, b):
        return pltpu.make_async_copy(send.at[t, g, b], big.at[g, 2 + b], recv_sem.at[g, b])

    def forward(side, slot, b):
        return pltpu.make_async_remote_copy(
            src_ref=big.at[slot, 2 + b],
            dst_ref=big.at[slot, 4 * side + b],
            send_sem=fsend_sem.at[side, slot, b],
            recv_sem=frecv_sem.at[side, slot, b],
            device_id=(t, left if side else right),
            device_id_type=MESH,
        )

    lane = lax.broadcasted_iota(jnp.int32, (CB, LANES), 1)
    lane_group = lane // BINS
    low_half = lane_group < 2
    even_part = lane_group % 2 == 0
    bin_row = lax.broadcasted_iota(jnp.int32, (1, NF), 1)
    count = jnp.minimum(bin_row + SMOOTH + 1, NF) - jnp.maximum(bin_row - SMOOTH, 0)
    inverse = 1.0 / count.astype(jnp.float32)

    def transform(g, b):
        rows = pl.ds(pl.multiple_of(b * CB, CB), CB)
        frames = jnp.concatenate(
            [
                xh[rows, pl.ds(pl.multiple_of(g * (JG * HALF) + jj * HALF, HALF), SEG)]
                for jj in range(JG)
            ],
            axis=0,
        )
        spec[...] = jnp.dot(frames, tab[...], preferred_element_type=jnp.float32)
        for jj in range(JG):
            part = pl.ds(jj * CB, CB)
            real = spec[part, pl.ds(0, NF)]
            imag = spec[part, pl.ds(NF, NF)]
            power = real * real + imag * imag
            head = power.astype(jnp.bfloat16)
            rest = (power - head.astype(jnp.float32)).astype(jnp.bfloat16)
            total = jnp.dot(head, ban[...], preferred_element_type=jnp.float32)
            total += jnp.dot(rest, ban[...], preferred_element_type=jnp.float32)
            scale = lax.rsqrt(total * inverse + whiten_eps)
            spec[part, pl.ds(0, NF)] = real * scale
            spec[part, pl.ds(NF, NF)] = imag * scale
        for q in range(2):
            for h in range(2):
                column = pl.ds(q * NF + h * LANES, LANES)
                tiles = [spec[pl.ds(jj * CB, CB), column] for jj in range(JG)]

                def swap(a, c, mask, by):
                    return (
                        jnp.where(mask, a, pltpu.roll(c, by, 1)),
                        jnp.where(mask, pltpu.roll(a, LANES - by, 1), c),
                    )

                t0, t2 = swap(tiles[0], tiles[2], low_half, 2 * BINS)
                t1, t3 = swap(tiles[1], tiles[3], low_half, 2 * BINS)
                u0, u1 = swap(t0, t1, even_part, BINS)
                u2, u3 = swap(t2, t3, even_part, BINS)
                for s, tile in enumerate((u0, u1, u2, u3)):
                    send[h * 4 + s, g, b, q] = tile.astype(jnp.bfloat16)

    def send_slot(slot):
        for b in range(2):
            run_copy(slot, b).start()

    def send_nearest(g, b):
        for i in range(2):
            run_copy(GROUPS + 2 * g + i, b).start()
        own_copy(g, b).start()

    for load in loads[:3]:
        load.wait()
    transform(jnp.int32(0), jnp.int32(0))
    for load in loads[4:]:
        load.start()
    pl.semaphore_wait(barrier, RUNS + 1)
    send_nearest(jnp.int32(0), 0)
    halo.start()
    loads[3].wait()
    transform(jnp.int32(0), jnp.int32(1))
    send_nearest(jnp.int32(0), 1)
    for load in loads[4:]:
        load.wait()

    def later_group(g, carry):
        @pl.when(g == GROUPS - 1)
        def _():
            halo.wait()

            @pl.when(t == RUNS - 1)
            def _():
                xh[:, pl.ds(samples, HALF)] = jnp.zeros((2 * CB, HALF), jnp.bfloat16)

        def block(b, inner):
            transform(g, b)
            send_nearest(g, b)
            return inner

        lax.fori_loop(0, 2, block, 0)
        return carry

    lax.fori_loop(1, GROUPS, later_group, 0)

    def send_more(slot, carry):
        send_slot(slot)
        return carry

    lax.fori_loop(3 * GROUPS, GROUPS + AHEAD, send_more, 0)

    base = edges[0, 0]
    bin_ids = lane % BINS
    for k in range(BANDS_DEV):
        inside = (bin_ids >= edges[0, k] - base) & (bin_ids < edges[1, k] - base)
        masks[k] = inside.astype(jnp.float32).astype(jnp.bfloat16)
    acc[...] = jnp.zeros_like(acc)

    def receive(slot):
        for b in range(2):
            run_copy(slot, b).wait_recv()
            forward(0, slot, b).start()
            forward(1, slot, b).start()

    def receive_own(g):
        for b in range(2):
            own_copy(g, b).wait()
            forward(0, g, b).start()
            forward(1, g, b).start()

    def wait_neighbours(first, depth):
        for b in range(2):
            for i in range(depth):
                for side in range(2):
                    forward(side, first + i, b).wait_recv()

    def multiply(first, depth, count, place_of):
        def one_left(item, carry):
            i = place_of(item)
            side = i // 4
            block = i - 2 * side
            base_right = 2 + 2 * side
            rights = jnp.concatenate(
                [
                    jnp.concatenate(
                        [big[first + p, base_right + n, q] for p in range(depth) for q in range(2)],
                        axis=1,
                    )
                    for n in range(2)
                ],
                axis=0,
            )
            for k in range(BANDS_DEV):
                mask = masks[k]
                pieces_re = []
                pieces_im = []
                for p in range(depth):
                    l0 = big[first + p, block, 0] * mask
                    l1 = big[first + p, block, 1] * mask
                    pieces_re += [l0, l1]
                    pieces_im += [l1, -l0]
                both = jnp.concatenate(
                    [jnp.concatenate(pieces_re, axis=1), jnp.concatenate(pieces_im, axis=1)], axis=0
                )
                sums = lax.dot_general(
                    both, rights, (((1,), (1,)), ((), ())), preferred_element_type=jnp.float32
                )
                for n in range(2):
                    for q in range(2):
                        acc[2 * i + n, k, q] += sums[q * CB:(q + 1) * CB, n * CB:(n + 1) * CB]
            return carry

        lax.fori_loop(0, count, one_left, 0)

    def multiply_own(first, depth):
        multiply(first, depth, 2, lambda item: item + 2)

    def multiply_neighbours(first, depth):
        wait_neighbours(first, depth)
        multiply(first, depth, 4, lambda item: item + 2 * (item // 2))

    def drain(slot, carry):
        for b in range(2):
            @pl.when(slot >= GROUPS)
            def _():
                run_copy(slot, b).wait_send()

            forward(0, slot, b).wait_send()
            forward(1, slot, b).wait_send()
        return carry

    def paired_step(unit, carry):
        first = 2 * unit
        for i in range(2):
            @pl.when(unit < GROUPS // 2)
            def _():
                receive_own(first + i)

            @pl.when(unit >= GROUPS // 2)
            def _():
                receive(first + i)

        @pl.when((first >= GROUPS) & (first + AHEAD < SLOTS))
        def _():
            for i in range(2):
                send_slot(first + AHEAD + i)

        multiply_own(first, 2)

        @pl.when(unit >= 1)
        def _():
            multiply_neighbours(first - 2, 2)

        @pl.when(first >= LATER)
        def _():
            for i in range(2):
                drain(first - LATER + i, 0)

        return carry

    lax.fori_loop(0, PAIRED // 2, paired_step, 0)
    receive(jnp.int32(PAIRED))
    multiply_own(PAIRED, 1)
    multiply_neighbours(PAIRED - 2, 2)

    def far_step(slot, carry):
        receive(slot)
        multiply_own(slot, 1)
        multiply_neighbours(slot - 1, 1)
        return carry

    lax.fori_loop(PAIRED + 1, SLOTS, far_step, 0)
    multiply_neighbours(SLOTS - 1, 1)
    lax.fori_loop(PAIRED - LATER, SLOTS, drain, 0)


def rows_kernel(edges, slots, acc, out, stage, out_sem):
    first_block = 2 * lax.axis_index("chan") - 2
    scales = []
    for k in range(BANDS_DEV):
        width = jnp.full((1, LANES), edges[1, k] - edges[0, k], jnp.int32).astype(jnp.float32)
        scales.append(1.0 / jnp.sqrt(128.0 * width))

    def row_copy(r):
        return pltpu.make_async_copy(stage.at[r], out.at[r], out_sem.at[r])

    def one_row(r, carry):
        a = slots[0, r]
        l = jnp.clip(a - first_block, 0, 3)
        n = jnp.clip(slots[1, r] - first_block, 2, 5)
        index = jnp.clip(jnp.where(n >= 4, 2 * (l + 2) + n - 4, 2 * l + n - 2), 0, 11)
        live = a >= 0
        for k in range(BANDS_DEV):
            for q in range(2):
                stage[r, k, q] = jnp.where(live, acc[index, k, q] * scales[k], 0.0)
        row_copy(r).start()
        return carry

    lax.fori_loop(0, ROWS, one_row, 0)
    for r in range(ROWS):
        row_copy(r).wait()


def shards(traces, band_edges, slot_pairs):
    tables, near = constant_tables()
    edges, slots = band_edges.T, slot_pairs.T
    smem = pl.BlockSpec(memory_space=pltpu.SMEM)
    vmem = pl.BlockSpec(memory_space=pltpu.VMEM)
    hbm = pl.BlockSpec(memory_space=pltpu.HBM)
    anywhere = pl.BlockSpec(memory_space=pl.ANY)
    bf16 = jnp.bfloat16
    traces = pltpu.with_memory_space_constraint(traces, pltpu.HBM)
    sums_shape = (12, BANDS_DEV, 2, CB, CB)
    sums = pl.pallas_call(
        cross_kernel,
        out_shape=pltpu.VMEM(sums_shape, jnp.float32),
        in_specs=[hbm, hbm, anywhere, anywhere],
        out_specs=vmem,
        scratch_shapes=[
            pltpu.SMEM((2, BANDS_DEV), jnp.int32),
            pltpu.VMEM((2 * CB, 4096 + HALF), bf16),
            pltpu.VMEM((SEG, 2 * NF), bf16),
            pltpu.VMEM((NF, NF), bf16),
            pltpu.VMEM((JG * CB, 2 * NF), jnp.float32),
            pltpu.VMEM((RUNS, GROUPS, 2, 2, CB, LANES), bf16),
            pltpu.VMEM((SLOTS, 6, 2, CB, LANES), bf16),
            pltpu.VMEM((BANDS_DEV, CB, LANES), bf16),
            pltpu.SemaphoreType.DMA((6,)),
            pltpu.SemaphoreType.DMA((2,)),
            pltpu.SemaphoreType.DMA((SLOTS, 2)),
            pltpu.SemaphoreType.DMA((SLOTS, 2)),
            pltpu.SemaphoreType.DMA((2, SLOTS, 2)),
            pltpu.SemaphoreType.DMA((2, SLOTS, 2)),
        ],
        compiler_params=pltpu.CompilerParams(
            collective_id=0, has_side_effects=True, vmem_limit_bytes=56 * 2**20
        ),
        name="cross_spectra",
    )(pltpu.with_memory_space_constraint(edges, pltpu.HBM), traces, tables, near)
    sums = pltpu.with_memory_space_constraint(sums, pltpu.VMEM)
    return pl.pallas_call(
        rows_kernel,
        out_shape=jax.ShapeDtypeStruct((ROWS, BANDS_DEV, 2, CB, CB), jnp.float32),
        in_specs=[smem, smem, vmem],
        out_specs=anywhere,
        scratch_shapes=[
            pltpu.VMEM((ROWS, BANDS_DEV, 2, CB, CB), jnp.float32),
            pltpu.SemaphoreType.DMA((ROWS,)),
        ],
        compiler_params=pltpu.CompilerParams(vmem_limit_bytes=16 * 2**20),
        name="output_rows",
    )(edges, slots, sums)


def solution(mesh):
    in_specs = (P("chan", "tm"), P("tm", None), P("chan", None))
    out_specs = P("chan", "tm", None, None, None)
    return jax.shard_map(shards, mesh=mesh, in_specs=in_specs, out_specs=out_specs, check_vma=False)
```
